32 devices in a mesh: occ: 16 (over z, y, x), vir: 2 (over core).
Axes of the slice: x: 2, y: 2, z: 4, core: 2. Of those that a mesh axis runs over, the one named last changes fastest.
Arguments:
- t2_tiles: float32 [16, 2, 4, 128, 256], P('occ', 'vir'), may hold values from -6 to 6
- cycle_ints: float32 [16, 2, 4, 256, 128], P('occ', 'vir'), may hold values from -0.21875 to 0.21875
- cycle_left: int32 [16, 2, 24], P('occ', 'vir'), may hold values from 0 to 3
- cycle_right: int32 [16, 2, 24], P('occ', 'vir'), may hold values from 0 to 3
- cycle_dest: int32 [16, 2, 24], P('occ', 'vir'), may hold values from 0 to 31, as said below
- lam_ladder: float32 [4096, 1024], P('occ', 'vir'), may hold values from -6 to 6
- ladder_ints: float32 [1024, 256], P('vir'), may hold values from -0.1875 to 0.1875
- ladder_mask: int32 [32, 8], P('occ', 'vir'), may hold values 0 or 1
- partner_slot: int32 [16, 2], P('occ'), may hold values from 0 to 1, as said below
- denom: float32 [4096, 256], P('occ', 'vir'), may hold values from 1 to 8
Outputs:
- increment: float32 [4096, 256], P('occ', 'vir')
The draws below stay inside these ranges and needn't reach their ends.
Inputs may be any that keep to these rules, and one draw needn't show every extreme that they name: One device's tasks name each owner (cycle_dest // 2) at most 3 times; in each vir column one owner is named exactly 3 times by every device. `partner_slot`: each row is a permutation of the 2 slots.
All inputs are finite; a program needn't handle non-finite values. No bound on the sum of `ladder_mask` on one device may be relied on, other than what follows from the above.
Results may differ from the reference program's by a relative error of at most 0.0001.
Values sent between devices are 32-bit elements; how exact they have to be, the bound alone decides.
A program may use at most 128 MiB of HBM per device.

```python
import math
import jax
import jax.numpy as jnp
from jax import lax

TILE = 128
OWN = 2
XT = 4
KC = 256
LB = 4
CAP = 3
TASKS = 24
N_OCC = 16
N_VIR = 2


def draw_cycle_dest(key, part):
    key_hot = jax.random.fold_in(key, 11)
    key_dev = jax.random.fold_in(key, 12)
    key_slot = jax.random.fold_in(key, 13)
    hot = jax.random.randint(key_hot, (N_VIR,), 0, N_OCC)
    hot_rep = jnp.tile(hot, N_OCC)
    keys = jax.random.split(key_dev, N_OCC * N_VIR)

    def single(device_key, hot_owner):
        key_pick, key_order = jax.random.split(device_key)
        others = jnp.arange((N_OCC - 1) * CAP, dtype=jnp.int32) // CAP
        others = others + (others >= hot_owner).astype(jnp.int32)
        picked = jax.random.permutation(key_pick, others)[:TASKS - CAP]
        owners = jnp.concatenate([jnp.full((CAP,), hot_owner, jnp.int32), picked])
        return jax.random.permutation(key_order, owners)
    owners = jax.vmap(single)(keys, hot_rep).reshape(N_OCC, N_VIR, TASKS)
    slots = jax.random.randint(key_slot, (N_OCC, N_VIR, TASKS), 0, OWN)
    return (owners * OWN + slots).astype(jnp.int32)


def draw_partner_slot(key, part):
    keys = jax.random.split(jax.random.fold_in(key, 21), N_OCC)

    def single(row_key):
        return jax.random.permutation(row_key, jnp.arange(OWN, dtype=jnp.int32))
    return jax.vmap(single)(keys).astype(jnp.int32)


def touch_ends(result, rng, least, high):
    longest = result.shape.index(max(result.shape))
    spots = []
    for shift in (0, 1):
        where = [jax.random.randint(jax.random.fold_in(rng, axis), (), 0, length) for axis, length in enumerate(result.shape)]
        where[longest] = (where[longest] + shift) % result.shape[longest]
        spots.append(tuple(where))
    return result.at[spots[0]].set(least).at[spots[1]].set(high)


def block_scale(rng, extent, shards, smallest, top_value):
    level = 1.0
    for position, blocks in shards:
        draws = jax.random.uniform(jax.random.fold_in(jax.random.fold_in(rng, 6), position), (blocks,), jnp.float32, smallest / len(shards), top_value / len(shards))
        level = level * jnp.repeat(jnp.exp(draws), extent[position] // blocks).reshape((-1,) + (1,) * (len(extent) - 1 - position))
    return level


def centred(key, extent, scale, limit, pieces=(), kind=jnp.bfloat16):
    drawn = jax.random.normal(key, extent, jnp.float32) * scale
    if len(pieces) > 0:
        drawn = block_scale(key, extent, pieces, -0.22, 0.18) * drawn
    return jnp.clip(drawn, min=-limit, max=limit).astype(kind)


def setup_inputs(seed: int = 0) -> dict:
    key_of = jax.random.split(jax.random.key(seed), 11)
    t2_tiles = centred(key_of[0], (N_OCC, N_VIR, XT, TILE, KC), 1.0, 6.0, ((0, 16), (1, 2)), jnp.float32)
    cycle_ints = centred(key_of[1], (N_OCC, N_VIR, XT, KC, TILE), (KC * CAP) ** -0.5, 0.21875, ((0, 16), (1, 2)), jnp.float32)
    cycle_left = touch_ends(jax.random.randint(key_of[2], (N_OCC, N_VIR, TASKS), 0, XT), jax.random.fold_in(key_of[2], 1), 0, XT - 1).astype(jnp.int32)
    cycle_right = touch_ends(jax.random.randint(key_of[3], (N_OCC, N_VIR, TASKS), 0, XT), jax.random.fold_in(key_of[3], 1), 0, XT - 1).astype(jnp.int32)
    cycle_dest = draw_cycle_dest(jax.random.fold_in(key_of[10], 71), 0)
    lam_ladder = centred(key_of[5], (N_OCC * OWN * TILE, N_VIR * LB * TILE), 1.0, 6.0, ((0, 16), (1, 2)), jnp.float32)
    ladder_ints = centred(key_of[6], (N_VIR * LB * TILE, N_VIR * TILE), (N_VIR * LB * TILE) ** -0.5, 0.1875, ((0, 2),), jnp.float32)
    ladder_mask = touch_ends((jax.random.randint(key_of[7], (N_OCC * OWN, N_VIR * LB), 0, 4) < 3).astype(jnp.int32), jax.random.fold_in(key_of[7], 1), 0, 1)
    partner_slot = draw_partner_slot(jax.random.fold_in(key_of[10], 71), 0)
    denom = jnp.clip(jnp.exp(math.log(8.0) - 2.0794415 * jax.random.uniform(key_of[9], (N_OCC * OWN * TILE, N_VIR * TILE), jnp.float32) ** block_scale(key_of[9], (N_OCC * OWN * TILE, N_VIR * TILE), ((0, 16), (1, 2)), -0.2, 0.2)), 1.0, 8.0)
    return {"t2_tiles": t2_tiles, "cycle_ints": cycle_ints, "cycle_left": cycle_left, "cycle_right": cycle_right, "cycle_dest": cycle_dest, "lam_ladder": lam_ladder, "ladder_ints": ladder_ints, "ladder_mask": ladder_mask, "partner_slot": partner_slot, "denom": denom}


def reference(t2_tiles, cycle_ints, cycle_left, cycle_right, cycle_dest, lam_ladder, ladder_ints, ladder_mask, partner_slot, denom):
    hi = lax.Precision.HIGHEST
    shaped = lam_ladder.reshape(N_OCC * OWN, TILE, N_VIR * LB, TILE)
    masked = (shaped * ladder_mask.astype(lam_ladder.dtype)[:, None, :, None]).reshape(N_OCC * OWN * TILE, N_VIR * LB * TILE)
    ladder = jnp.dot(masked, ladder_ints, precision=hi)

    def column(q):
        def step(acc, p):
            xs = t2_tiles[p, q]
            ys = cycle_ints[p, q]
            part = jnp.einsum("btk,bkc->btc", xs[cycle_left[p, q]], ys[cycle_right[p, q]], precision=hi)
            return acc + jax.ops.segment_sum(part, cycle_dest[p, q], num_segments=N_OCC * OWN), None
        start = jnp.zeros((N_OCC * OWN, TILE, TILE), t2_tiles.dtype)
        return lax.scan(step, start, jnp.arange(N_OCC, dtype=jnp.int32))[0]

    cycle = lax.map(column, jnp.arange(N_VIR, dtype=jnp.int32))
    cycle = cycle.transpose(1, 2, 0, 3).reshape(N_OCC * OWN * TILE, N_VIR * TILE)
    resid = (ladder + cycle).reshape(N_OCC, OWN, TILE, N_VIR, TILE)
    flipped = resid[::-1]
    partner = jnp.take_along_axis(flipped, partner_slot[:, :, None, None, None], axis=1)
    partner = partner[:, :, ::-1, :, ::-1]
    sym = (resid + partner).reshape(N_OCC * OWN * TILE, N_VIR * TILE)
    return sym / denom
```

```python
import functools

import jax
import jax.numpy as jnp
from jax import lax
from jax.experimental import pallas as pl
from jax.experimental.pallas import tpu as pltpu
from jax.sharding import PartitionSpec as P

CAP = 3
MESH = pl.DeviceIdType.MESH
f32 = jnp.float32
bf16 = jnp.bfloat16


def split2(x):
    hi = x.astype(bf16)
    return hi, (x - hi.astype(f32)).astype(bf16)


def dot(a, b):
    return jnp.dot(a, b, preferred_element_type=f32)


def dot3(a, b):
    return dot(a[0], b[0]) + (dot(a[0], b[1]) + dot(a[1], b[0]))


def toggle(value, bit, on=1):
    return value + on * bit * (1 - 2 * ((value // bit) % 2))


def chunk_plan(edge):
    unit = edge // 2 // 8
    big = unit // 3 + unit % 3 // 2
    sizes = [big * 8, big * 8, (unit - 2 * big) * 8]
    return [(sum(sizes[:c]), sizes[c]) for c in range(3)]


def kernel(
    n_occ, n_vir, chunks,
    left, right, dest, mask, slot, t2_hbm, ints_hbm, lam_hbm, lints_hbm,
    out,
    t2, ints, lam, lints, code_v, code_s, prod, lam_hi, lam_lo, lad, lad_got, flag, flag_got,
    c0, c1, c2, r0, r1, r2, s0, s1, s2, t0, t1, t2s, g0, g1, g2, w0, w1, w2,
    load_sem, code_sem, send_sem, recv_sem, fin_send, fin_recv, lad_send, lad_recv, flag_send, flag_recv,
):
    acc, got, own, fin, fin_got, flips = (c0, c1, c2), (r0, r1, r2), (s0, s1, s2), (t0, t1, t2s), (g0, g1, g2), (w0, w1, w2)
    edge = prod.shape[1]
    xt = t2.shape[0]
    owned = 2
    count = dest.shape[2]
    bits = n_occ.bit_length() - 1
    levels = bits - 1
    blocks = n_occ // 2
    width = (xt * xt).bit_length()
    p = lax.axis_index("occ")
    q = lax.axis_index("vir")
    upper = p // blocks
    cls = p + upper * (n_occ - 1 - 2 * p)
    partner = n_occ - 1 - p
    orders = [[1 << ((c + levels - 1 - h) % levels) for h in range(levels)] for c in range(3)]

    loads = [
        pltpu.make_async_copy(src, dst, load_sem.at[i])
        for i, (src, dst) in enumerate(
            ((t2_hbm.at[0, 0], t2), (ints_hbm.at[0, 0], ints), (lam_hbm, lam), (lints_hbm, lints))
        )
    ]
    for load in loads:
        load.start()

    barrier = pltpu.get_barrier_semaphore()
    for b in range(levels):
        pl.semaphore_signal(barrier, inc=1, device_id=(toggle(p, 1 << b), q), device_id_type=MESH)
    pl.semaphore_signal(barrier, inc=1, device_id=(partner, q), device_id_type=MESH)
    for off in range(1, n_vir):
        pl.semaphore_signal(barrier, inc=1, device_id=(p, (q + off) % n_vir), device_id_type=MESH)

    tile_id = lax.broadcasted_iota(jnp.int32, code_v.shape, 0) * 128 + lax.broadcasted_iota(
        jnp.int32, code_v.shape, 1
    )

    def note(t, packed):
        code = left[0, 0, t] * xt + right[0, 0, t] + 1
        return jnp.where(tile_id == dest[0, 0, t], packed * (1 << width) + code, packed)

    code_v[...] = lax.fori_loop(0, count, note, jnp.zeros(code_v.shape, jnp.int32))
    codes = pltpu.make_async_copy(code_v, code_s, code_sem)
    codes.start()
    flag[...] = jnp.full(flag.shape, slot[0, 0], jnp.int32)
    prod[0] = jnp.zeros((edge, edge), f32)

    loads[0].wait()
    loads[1].wait()
    a = split2(t2[...].reshape(xt * edge, t2.shape[2]))
    for r in range(0, xt, 2):
        b = split2(jnp.concatenate([ints[r], ints[r + 1]], axis=1))
        res = dot3(a, b)
        for l in range(xt):
            for d in range(2):
                prod[1 + l * xt + r + d] = res[l * edge : (l + 1) * edge, d * edge : (d + 1) * edge]
    codes.wait()

    def assemble(c, i):
        lo, half = chunks[c]
        home = cls
        for h in range(levels):
            home = toggle(home, orders[c][h], (i // (1 << h)) % 2)
        for j in range(2 * owned):
            owner = home if j < owned else n_occ - 1 - home
            g = owner * owned + j % owned
            packed = code_s[g // 128, g % 128]
            ids = [lax.shift_right_logical(packed, width * k) & ((1 << width) - 1) for k in range(CAP)]
            for at, row in ((0, lo), (half, edge - lo - half)):
                tiles = [prod[k, row : row + half, :] for k in ids]
                acc[c][i, j, at : at + half, :] = tiles[0] + tiles[1] + tiles[2]

    def step_copy(c, i, h):
        return pltpu.make_async_remote_copy(
            src_ref=acc[c].at[i],
            dst_ref=got[c].at[i],
            send_sem=send_sem.at[c, i],
            recv_sem=recv_sem.at[c, i],
            device_id=(toggle(p, orders[c][h]), q),
            device_id_type=MESH,
        )

    pl.semaphore_wait(barrier, bits + n_vir - 1)
    flag_copy = pltpu.make_async_remote_copy(
        src_ref=flag, dst_ref=flag_got, send_sem=flag_send, recv_sem=flag_recv,
        device_id=(partner, q), device_id_type=MESH,
    )
    flag_copy.start()

    top = blocks // 2

    @pl.loop(0, top)
    def _(n):
        i = blocks - 1 - n
        for c in range(3):
            assemble(c, i)
            step_copy(c, i, levels - 1).start()

    @pl.loop(0, top)
    def _(n):
        for c in range(3):
            assemble(c, top - 1 - n)

    loads[2].wait()
    loads[3].wait()
    for s in range(owned):
        for b in range(mask.shape[1]):
            rows, cols = pl.ds(s * edge, edge), pl.ds(b * edge, edge)
            hi, lo = split2(lam[rows, cols] * mask[s, b].astype(f32))
            lam_hi[rows, cols] = hi
            lam_lo[rows, cols] = lo

    def ladder(column):
        cols = pl.ds(pl.multiple_of(column * edge, edge), edge)
        return dot3((lam_hi[...], lam_lo[...]), split2(lints[:, cols]))

    lad_copies = []
    for off in range(1, n_vir):
        column = (q + off) % n_vir
        lad[off] = ladder(column)
        lad_copies.append(
            pltpu.make_async_remote_copy(
                src_ref=lad.at[off], dst_ref=lad_got.at[off - 1],
                send_sem=lad_send.at[off - 1], recv_sem=lad_recv.at[off - 1],
                device_id=(p, column), device_id_type=MESH,
            )
        )
        lad_copies[-1].start()
    lad[0] = ladder(q)

    def take(c, i, h):
        for k in range(h, levels):
            step_copy(c, i + (1 << k), k).wait_recv()
            acc[c][i] = acc[c][i] + got[c][i + (1 << k)]

    for h in reversed(range(levels - 1)):

        @pl.loop(0, 1 << h)
        def _(n):
            i = 2 * (1 << h) - 1 - n
            for c in range(3):
                take(c, i, h + 1)
                step_copy(c, i, h).start()

    for copy in lad_copies:
        copy.wait_recv()
    total = lad[0]
    for off in range(1, n_vir):
        total = total + lad_got[off - 1]
    lad[0] = total
    flag_copy.wait_recv()
    lanes = lax.broadcasted_iota(jnp.int32, (edge, edge), 0) + lax.broadcasted_iota(jnp.int32, (edge, edge), 1)
    turn_lanes = jnp.where(lanes == edge - 1, 1.0, 0.0).astype(bf16)

    def fin_copy(c):
        return pltpu.make_async_remote_copy(
            src_ref=fin[c], dst_ref=fin_got[c], send_sem=fin_send.at[c], recv_sem=fin_recv.at[c],
            device_id=(partner, q), device_id_type=MESH,
        )

    for c in range(3):
        lo, half = chunks[c]
        m = 2 * half
        take(c, 0, 0)
        for s in range(owned):
            j = upper * owned + s
            for at, row in ((0, lo), (half, edge - lo - half)):
                here = pl.ds(at, half)
                acc[c][0, j, here, :] = acc[c][0, j, here, :] + lad[0, s * edge + row : s * edge + row + half, :]
        x = acc[c][0].reshape(4 * m, edge)
        hi, rest = split2(x)
        mid, low = split2(x - hi.astype(f32))
        size = 4 * m
        rows = lax.broadcasted_iota(jnp.int32, (size, size), 0) + lax.broadcasted_iota(jnp.int32, (size, size), 1)
        turn_rows = jnp.where(rows == size - 1, 1.0, 0.0).astype(bf16)
        y = None
        for piece in (hi, mid, low):
            part = dot(turn_rows, dot(piece, turn_lanes).astype(bf16))
            y = part if y is None else y + part
        flips[c][...] = y.reshape(4, m, edge)
        for target, which, swap in ((fin[c], 1 - upper, flag_got), (own[c], upper, flag)):
            first = flips[c][2 * which + 1]
            second = flips[c][2 * which]
            keep = jnp.broadcast_to(swap[0:1, :] == 0, (m, edge))
            target[0] = acc[c][0, 2 * which] + jnp.where(keep, first, second)
            target[1] = acc[c][0, 2 * which + 1] + jnp.where(keep, second, first)
            if target is fin[c]:
                fin_copy(c).start()

    for c in range(3):
        lo, half = chunks[c]
        fin_copy(c).wait_recv()
        for s in range(owned):
            for at, row in ((0, lo), (half, edge - lo - half)):
                out[s * edge + row : s * edge + row + half, :] = (
                    own[c][s, at : at + half, :] + fin_got[c][s, at : at + half, :]
                )

    flag_copy.wait_send()
    for copy in lad_copies:
        copy.wait_send()
    for c in range(3):
        fin_copy(c).wait_send()
        for h in range(levels):

            @pl.loop(1 << h, 2 << h)
            def _(i):
                step_copy(c, i, h).wait_send()


def body(
    n_occ, n_vir,
    t2_tiles, cycle_ints, cycle_left, cycle_right, cycle_dest, lam_ladder, ladder_ints, ladder_mask, partner_slot, denom,
):
    edge = denom.shape[1]
    owned = partner_slot.shape[1]
    xt, kc = cycle_ints.shape[2], cycle_ints.shape[3]
    blocks = n_occ // 2
    chunks = chunk_plan(edge)
    tiles = n_occ * owned
    code_rows = -(-tiles // 128)
    rows = owned * edge
    per_chunk = lambda *lead: [pltpu.VMEM((*lead, 2 * half, edge), f32) for _, half in chunks]
    sem = pltpu.SemaphoreType.DMA
    smem = pl.BlockSpec(memory_space=pltpu.SMEM)
    hbm = pl.BlockSpec(memory_space=pl.ANY)
    sym = pl.pallas_call(
        functools.partial(kernel, n_occ, n_vir, chunks),
        out_shape=jax.ShapeDtypeStruct((rows, edge), f32),
        in_specs=[smem] * 5 + [hbm] * 4,
        out_specs=pl.BlockSpec(memory_space=pltpu.VMEM),
        scratch_shapes=[
            pltpu.VMEM((xt, edge, kc), f32),
            pltpu.VMEM((xt, kc, edge), f32),
            pltpu.VMEM(lam_ladder.shape, f32),
            pltpu.VMEM(ladder_ints.shape, f32),
            pltpu.VMEM((code_rows, 128), jnp.int32),
            pltpu.SMEM((code_rows, 128), jnp.int32),
            pltpu.VMEM((1 + xt * xt, edge, edge), f32),
            pltpu.VMEM(lam_ladder.shape, bf16),
            pltpu.VMEM(lam_ladder.shape, bf16),
            pltpu.VMEM((n_vir, rows, edge), f32),
            pltpu.VMEM((n_vir - 1, rows, edge), f32),
            pltpu.VMEM((8, 128), jnp.int32),
            pltpu.VMEM((8, 128), jnp.int32),
            *per_chunk(blocks, 2 * owned),
            *per_chunk(blocks, 2 * owned),
            *per_chunk(owned),
            *per_chunk(owned),
            *per_chunk(owned),
            *per_chunk(2 * owned),
            sem((4,)),
            sem,
            sem((3, blocks)),
            sem((3, blocks)),
            sem((3,)),
            sem((3,)),
            sem((n_vir - 1,)),
            sem((n_vir - 1,)),
            sem,
            sem,
        ],
        compiler_params=pltpu.CompilerParams(
            collective_id=0, has_side_effects=True, vmem_limit_bytes=40 * 1024 * 1024
        ),
        cost_estimate=pl.CostEstimate(flops=10**9, bytes_accessed=4 * 10**6, transcendentals=0),
    )(cycle_left, cycle_right, cycle_dest, ladder_mask, partner_slot, t2_tiles, cycle_ints, lam_ladder, ladder_ints)
    return sym / denom


def solution(mesh):
    in_specs = (
        P("occ", "vir", None, None, None),
        P("occ", "vir", None, None, None),
        P("occ", "vir", None),
        P("occ", "vir", None),
        P("occ", "vir", None),
        P("occ", "vir"),
        P("vir", None),
        P("occ", "vir"),
        P("occ", None),
        P("occ", "vir"),
    )
    local = functools.partial(body, mesh.shape["occ"], mesh.shape["vir"])
    return jax.shard_map(local, mesh=mesh, in_specs=in_specs, out_specs=P("occ", "vir"), check_vma=False)
```

```python
import functools

import jax
import jax.numpy as jnp
from jax import lax
from jax.experimental import pallas as pl
from jax.experimental.pallas import tpu as pltpu
from jax.sharding import PartitionSpec as P

CAP = 3
MESH = pl.DeviceIdType.MESH
f32 = jnp.float32
bf16 = jnp.bfloat16


def split2(x):
    hi = x.astype(bf16)
    return hi, (x - hi.astype(f32)).astype(bf16)


def dot(a, b):
    return jnp.dot(a, b, preferred_element_type=f32)


def dot3(a, b):
    return dot(a[0], b[0]) + (dot(a[0], b[1]) + dot(a[1], b[0]))


def toggle(value, bit, on=1):
    return value + on * bit * (1 - 2 * ((value // bit) % 2))


def chunk_plan(edge):
    unit = edge // 2 // 8
    big = unit // 3 + unit % 3 // 2
    sizes = [big * 8, big * 8, (unit - 2 * big) * 8]
    return [(sum(sizes[:c]), sizes[c]) for c in range(3)]


def turned(matrix, x):
    return dot(matrix, x).astype(bf16)


def split3(x):
    hi, rest = split2(x)
    mid, low = split2(x - hi.astype(f32))
    return hi, mid, low


def permutation(size, reverse):
    row = lax.broadcasted_iota(jnp.int32, (size, size), 0)
    col = lax.broadcasted_iota(jnp.int32, (size, size), 1)
    target = row + reverse * (size - 1 - 2 * row)
    return jnp.where(target == col, 1.0, 0.0).astype(bf16)


def kernel(
    n_occ, n_vir, chunks,
    left_hbm, right_hbm, dest_hbm, mask_hbm, slot_hbm, t2_hbm, ints_hbm, lam_hbm, lints_hbm,
    out,
    left, right, dest, mask, slot,
    t2, ints, lam, lints, code_v, code_s, prod, lam_hi, lam_lo, lad, lad_got, flag, flag_got,
    c0, c1, c2, r0, r1, r2, s0, s1, s2, t0, t1, t2s, g0, g1, g2, w0, w1, w2,
    load_sem, code_sem, send_sem, recv_sem, fin_send, fin_recv, lad_send, lad_recv, flag_send, flag_recv,
):
    acc, got, own, fin, fin_got, flips = (c0, c1, c2), (r0, r1, r2), (s0, s1, s2), (t0, t1, t2s), (g0, g1, g2), (w0, w1, w2)
    edge = prod.shape[1]
    xt = t2.shape[0]
    pairs = xt * xt
    owned = 2
    count = dest.shape[2]
    bits = n_occ.bit_length() - 1
    levels = bits - 1
    blocks = n_occ // 2
    width = pairs.bit_length()
    p = lax.axis_index("occ")
    q = lax.axis_index("vir")
    upper = p // blocks
    cls = p + upper * (n_occ - 1 - 2 * p)
    partner = n_occ - 1 - p
    orders = [[1 << ((c + levels - 1 - h) % levels) for h in range(levels)] for c in range(3)]

    loads = [
        pltpu.make_async_copy(src, dst, load_sem.at[i])
        for i, (src, dst) in enumerate(
            (
                (left_hbm, left), (right_hbm, right), (dest_hbm, dest), (slot_hbm, slot),
                (t2_hbm.at[0, 0], t2), (ints_hbm.at[0, 0], ints),
                (mask_hbm, mask), (lam_hbm, lam), (lints_hbm, lints),
            )
        )
    ]
    for load in loads:
        load.start()

    barrier = pltpu.get_barrier_semaphore()
    for b in range(levels):
        pl.semaphore_signal(barrier, inc=1, device_id=(toggle(p, 1 << b), q), device_id_type=MESH)
    pl.semaphore_signal(barrier, inc=1, device_id=(partner, q), device_id_type=MESH)
    for off in range(1, n_vir):
        pl.semaphore_signal(barrier, inc=1, device_id=(p, (q + off) % n_vir), device_id_type=MESH)

    tile_id = lax.broadcasted_iota(jnp.int32, code_v.shape, 0) * 128 + lax.broadcasted_iota(
        jnp.int32, code_v.shape, 1
    )
    for load in loads[:4]:
        load.wait()

    def note(t, packed):
        code = left[0, 0, t] * xt + right[0, 0, t] + 1
        return jnp.where(tile_id == dest[0, 0, t], packed * (1 << width) + code, packed)

    code_v[...] = lax.fori_loop(0, count, note, jnp.zeros(code_v.shape, jnp.int32))
    codes = pltpu.make_async_copy(code_v, code_s, code_sem)
    codes.start()
    flag[...] = jnp.full(flag.shape, slot[0, 0], jnp.int32)

    prod[0] = jnp.zeros((edge, edge), f32)
    prod[1 + pairs] = jnp.zeros((edge, edge), f32)
    turn = permutation(edge, 1)
    loads[4].wait()
    loads[5].wait()
    a = split2(t2[...].reshape(xt * edge, t2.shape[2]))
    a_turned = [
        jnp.concatenate([turned(turn, x[l * edge : (l + 1) * edge]) for l in range(xt)], axis=0) for x in a
    ]
    for r in range(0, xt, 2):
        sides = [split2(ints[r + d]) for d in range(2)]
        b = [jnp.concatenate([sides[0][k], sides[1][k]], axis=1) for k in range(2)]
        b_turned = [
            jnp.concatenate([turned(sides[0][k], turn), turned(sides[1][k], turn)], axis=1) for k in range(2)
        ]
        for base, res in ((1, dot3(a, b)), (2 + pairs, dot3(a_turned, b_turned))):
            for l in range(xt):
                for d in range(2):
                    prod[base + l * xt + r + d] = res[l * edge : (l + 1) * edge, d * edge : (d + 1) * edge]
    codes.wait()

    def assemble(c, i):
        lo, half = chunks[c]
        home = cls
        for h in range(levels):
            home = toggle(home, orders[c][h], (i // (1 << h)) % 2)
        ids = []
        for j in range(2 * owned):
            g = (home if j < owned else n_occ - 1 - home) * owned + j % owned
            packed = code_s[g // 128, g % 128]
            base = 0 if j < owned else 1 + pairs
            ids.append([base + (lax.shift_right_logical(packed, width * k) & ((1 << width) - 1)) for k in range(CAP)])
        for at, row in ((0, lo), (half, edge - lo - half)):
            low0, low1, up0, up1 = [
                prod[k[0], row : row + half, :] + prod[k[1], row : row + half, :] + prod[k[2], row : row + half, :]
                for k in ids
            ]
            acc[c][i, 0, at : at + half, :] = low0 + up0
            acc[c][i, 1, at : at + half, :] = low0 + up1
            acc[c][i, 2, at : at + half, :] = low1 + up0

    def step_copy(c, i, h):
        return pltpu.make_async_remote_copy(
            src_ref=acc[c].at[i],
            dst_ref=got[c].at[i],
            send_sem=send_sem.at[c, i],
            recv_sem=recv_sem.at[c, i],
            device_id=(toggle(p, orders[c][h]), q),
            device_id_type=MESH,
        )

    pl.semaphore_wait(barrier, bits + n_vir - 1)

    top = blocks // 2

    @pl.loop(0, top)
    def _(n):
        i = blocks - 1 - n
        for c in range(3):
            assemble(c, i)
            step_copy(c, i, levels - 1).start()

    flag_copy = pltpu.make_async_remote_copy(
        src_ref=flag, dst_ref=flag_got, send_sem=flag_send, recv_sem=flag_recv,
        device_id=(partner, q), device_id_type=MESH,
    )
    flag_copy.start()

    @pl.loop(0, top)
    def _(n):
        for c in range(3):
            assemble(c, top - 1 - n)

    for load in loads[6:]:
        load.wait()
    for s in range(owned):
        for b in range(mask.shape[1]):
            rows, cols = pl.ds(s * edge, edge), pl.ds(b * edge, edge)
            hi, lo = split2(lam[rows, cols] * mask[s, b].astype(f32))
            lam_hi[rows, cols] = hi
            lam_lo[rows, cols] = lo

    def ladder(column):
        cols = pl.ds(pl.multiple_of(column * edge, edge), edge)
        return dot3((lam_hi[...], lam_lo[...]), split2(lints[:, cols]))

    lad_copies = []
    for off in range(1, n_vir):
        column = (q + off) % n_vir
        lad[off] = ladder(column)
        lad_copies.append(
            pltpu.make_async_remote_copy(
                src_ref=lad.at[off], dst_ref=lad_got.at[off - 1],
                send_sem=lad_send.at[off - 1], recv_sem=lad_recv.at[off - 1],
                device_id=(p, column), device_id_type=MESH,
            )
        )
        lad_copies[-1].start()
    lad[0] = ladder(q)
    lanes = permutation(edge, upper)

    def add_ladder():
        for copy in lad_copies:
            copy.wait_recv()
        total = lad[0]
        for off in range(1, n_vir):
            total = total + lad_got[off - 1]
        for s in range(owned):
            y = None
            for piece in split3(total[s * edge : (s + 1) * edge]):
                part = dot(lanes, turned(piece, lanes))
                y = part if y is None else y + part
            lad[0, s * edge : (s + 1) * edge, :] = y
        for c in range(3):
            lo, half = chunks[c]
            for at, row in ((0, lo), (half, edge - lo - half)):
                here = pl.ds(at, half)
                for j, s in ((0, 0), (1, upper), (2, 1 - upper)):
                    acc[c][0, j, here, :] = acc[c][0, j, here, :] + lad[0, pl.ds(pl.multiple_of(s * edge + row, 8), half), :]

    def take(c, i, h):
        for k in range(h, levels):
            step_copy(c, i + (1 << k), k).wait_recv()
            acc[c][i] = acc[c][i] + got[c][i + (1 << k)]

    for h in reversed(range(levels - 1)):
        if h == 0:
            add_ladder()

        @pl.loop(0, 1 << h)
        def _(n):
            i = 2 * (1 << h) - 1 - n
            for c in range(3):
                take(c, i, h + 1)
                step_copy(c, i, h).start()

    flag_copy.wait_recv()

    def fin_copy(c):
        return pltpu.make_async_remote_copy(
            src_ref=fin[c], dst_ref=fin_got[c], send_sem=fin_send.at[c], recv_sem=fin_recv.at[c],
            device_id=(partner, q), device_id_type=MESH,
        )

    for c in range(3):
        m = 2 * chunks[c][1]
        take(c, 0, 0)
        for target, which, swap in ((fin[c], 1 - upper, flag_got), (own[c], upper, flag)):
            keep = jnp.broadcast_to(swap[0:1, :] == 0, (m, edge))
            first, second = acc[c][0, 1 + which], acc[c][0, 2 - which]
            target[0] = jnp.where(keep, acc[c][0, 0], first)
            target[1] = jnp.where(keep, (first - acc[c][0, 0]) + second, second)
            if target is fin[c]:
                fin_copy(c).start()

    for c in range(3):
        lo, half = chunks[c]
        size = 2 * owned * half
        rows = permutation(size, upper)
        fin_copy(c).wait_recv()
        y = None
        for piece in split3((own[c][...] + fin_got[c][...]).reshape(size, edge)):
            part = dot(rows, turned(piece, lanes))
            y = part if y is None else y + part
        flips[c][...] = y.reshape(owned, 2 * half, edge)
        for s in range(owned):
            for at, row in ((0, lo), (half, edge - lo - half)):
                out[s * edge + row : s * edge + row + half, :] = flips[c][s + upper * (1 - 2 * s), at : at + half, :]

    flag_copy.wait_send()
    for copy in lad_copies:
        copy.wait_send()
    for c in range(3):
        fin_copy(c).wait_send()
        for h in range(levels):

            @pl.loop(1 << h, 2 << h)
            def _(i):
                step_copy(c, i, h).wait_send()


def body(
    n_occ, n_vir,
    t2_tiles, cycle_ints, cycle_left, cycle_right, cycle_dest, lam_ladder, ladder_ints, ladder_mask, partner_slot, denom,
):
    edge = denom.shape[1]
    owned = partner_slot.shape[1]
    xt, kc = cycle_ints.shape[2], cycle_ints.shape[3]
    blocks = n_occ // 2
    chunks = chunk_plan(edge)
    tiles = n_occ * owned
    code_rows = -(-tiles // 128)
    rows = owned * edge
    per_chunk = lambda *lead: [pltpu.VMEM((*lead, 2 * half, edge), f32) for _, half in chunks]
    sem = pltpu.SemaphoreType.DMA
    hbm = pl.BlockSpec(memory_space=pltpu.HBM)
    smem = lambda x: pltpu.SMEM(x.shape, x.dtype)
    sym = pl.pallas_call(
        functools.partial(kernel, n_occ, n_vir, chunks),
        out_shape=jax.ShapeDtypeStruct((rows, edge), f32),
        in_specs=[hbm] * 9,
        out_specs=pl.BlockSpec(memory_space=pltpu.VMEM),
        scratch_shapes=[
            smem(cycle_left),
            smem(cycle_right),
            smem(cycle_dest),
            smem(ladder_mask),
            smem(partner_slot),
            pltpu.VMEM((xt, edge, kc), f32),
            pltpu.VMEM((xt, kc, edge), f32),
            pltpu.VMEM(lam_ladder.shape, f32),
            pltpu.VMEM(ladder_ints.shape, f32),
            pltpu.VMEM((code_rows, 128), jnp.int32),
            pltpu.SMEM((code_rows, 128), jnp.int32),
            pltpu.VMEM((2 + 2 * xt * xt, edge, edge), f32),
            pltpu.VMEM(lam_ladder.shape, bf16),
            pltpu.VMEM(lam_ladder.shape, bf16),
            pltpu.VMEM((n_vir, rows, edge), f32),
            pltpu.VMEM((n_vir - 1, rows, edge), f32),
            pltpu.VMEM((8, 128), jnp.int32),
            pltpu.VMEM((8, 128), jnp.int32),
            *per_chunk(blocks, 3),
            *per_chunk(blocks, 3),
            *per_chunk(owned),
            *per_chunk(owned),
            *per_chunk(owned),
            *per_chunk(owned),
            sem((9,)),
            sem,
            sem((3, blocks)),
            sem((3, blocks)),
            sem((3,)),
            sem((3,)),
            sem((n_vir - 1,)),
            sem((n_vir - 1,)),
            sem,
            sem,
        ],
        compiler_params=pltpu.CompilerParams(
            collective_id=0, has_side_effects=True, vmem_limit_bytes=62 * 1024 * 1024
        ),
        cost_estimate=pl.CostEstimate(flops=10**9, bytes_accessed=4 * 10**6, transcendentals=0),
    )(cycle_left, cycle_right, cycle_dest, ladder_mask, partner_slot, t2_tiles, cycle_ints, lam_ladder, ladder_ints)
    return sym / denom


def solution(mesh):
    in_specs = (
        P("occ", "vir", None, None, None),
        P("occ", "vir", None, None, None),
        P("occ", "vir", None),
        P("occ", "vir", None),
        P("occ", "vir", None),
        P("occ", "vir"),
        P("vir", None),
        P("occ", "vir"),
        P("occ", None),
        P("occ", "vir"),
    )
    local = functools.partial(body, mesh.shape["occ"], mesh.shape["vir"])
    return jax.shard_map(local, mesh=mesh, in_specs=in_specs, out_specs=P("occ", "vir"), check_vma=False)
```

```python
import functools

import jax
import jax.numpy as jnp
from jax import lax
from jax.experimental import pallas as pl
from jax.experimental.pallas import tpu as pltpu
from jax.sharding import PartitionSpec as P

CAP = 3
MESH = pl.DeviceIdType.MESH
f32 = jnp.float32
bf16 = jnp.bfloat16


def split2(x):
    hi = x.astype(bf16)
    return hi, (x - hi.astype(f32)).astype(bf16)


def dot(a, b):
    return jnp.dot(a, b, preferred_element_type=f32)


def dot3(a, b):
    return dot(a[0], b[0]) + (dot(a[0], b[1]) + dot(a[1], b[0]))


def toggle(value, bit, on=1):
    return value + on * bit * (1 - 2 * ((value // bit) % 2))


CHUNKS = 6
AXES = 3


def chunk_plan(edge):
    sizes = [units * (edge // 16) for units in (2, 2, 1, 1, 1, 1)]
    return [(sum(sizes[:c]), sizes[c]) for c in range(CHUNKS)]


def turned(matrix, x):
    return dot(matrix, x).astype(bf16)


def split3(x):
    hi, rest = split2(x)
    mid, low = split2(x - hi.astype(f32))
    return hi, mid, low


def permutation(size, reverse):
    row = lax.broadcasted_iota(jnp.int32, (size, size), 0)
    col = lax.broadcasted_iota(jnp.int32, (size, size), 1)
    target = row + reverse * (size - 1 - 2 * row)
    return jnp.where(target == col, 1.0, 0.0).astype(bf16)


def kernel(
    n_occ, n_vir, chunks,
    left_hbm, right_hbm, dest_hbm, mask_hbm, slot_hbm, t2_hbm, ints_hbm, lam_hbm, lints_hbm,
    out,
    left, right, dest, mask, slot,
    t2, ints, lam, lints, code_v, code_s, prod, lam_hi, lam_lo, lad, lad_got, flag, flag_got,
    per_chunk,
    load_sem, code_sem, send_sem, recv_sem, fin_send, fin_recv, lad_send, lad_recv, flag_send, flag_recv,
):
    acc, got, own, fin, fin_got, flips = per_chunk
    edge = prod.shape[1]
    xt = t2.shape[0]
    pairs = xt * xt
    owned = 2
    count = dest.shape[2]
    bits = n_occ.bit_length() - 1
    levels = bits - 1
    blocks = n_occ // 2
    width = pairs.bit_length()
    p = lax.axis_index("occ")
    q = lax.axis_index("vir")
    upper = p // blocks
    cls = p + upper * (n_occ - 1 - 2 * p)
    partner = n_occ - 1 - p
    orders = [[1 << ((c % AXES + levels - 1 - h) % levels) for h in range(levels)] for c in range(CHUNKS)]
    early, late = range(AXES), range(AXES, CHUNKS)

    loads = [
        pltpu.make_async_copy(src, dst, load_sem.at[i])
        for i, (src, dst) in enumerate(
            (
                (left_hbm, left), (right_hbm, right), (dest_hbm, dest), (slot_hbm, slot),
                (t2_hbm.at[0, 0], t2), (ints_hbm.at[0, 0], ints),
                (mask_hbm, mask), (lam_hbm, lam), (lints_hbm, lints),
            )
        )
    ]
    for load in loads:
        load.start()

    barrier = pltpu.get_barrier_semaphore()
    for b in range(levels):
        pl.semaphore_signal(barrier, inc=1, device_id=(toggle(p, 1 << b), q), device_id_type=MESH)
    pl.semaphore_signal(barrier, inc=1, device_id=(partner, q), device_id_type=MESH)
    for off in range(1, n_vir):
        pl.semaphore_signal(barrier, inc=1, device_id=(p, (q + off) % n_vir), device_id_type=MESH)

    tile_id = lax.broadcasted_iota(jnp.int32, code_v.shape, 0) * 128 + lax.broadcasted_iota(
        jnp.int32, code_v.shape, 1
    )
    for load in loads[:4]:
        load.wait()

    def note(t, packed):
        code = left[0, 0, t] * xt + right[0, 0, t] + 1
        return jnp.where(tile_id == dest[0, 0, t], packed * (1 << width) + code, packed)

    code_v[...] = lax.fori_loop(0, count, note, jnp.zeros(code_v.shape, jnp.int32))
    codes = pltpu.make_async_copy(code_v, code_s, code_sem)
    codes.start()
    flag[...] = jnp.full(flag.shape, slot[0, 0], jnp.int32)

    prod[0] = jnp.zeros((edge, edge), f32)
    prod[1 + pairs] = jnp.zeros((edge, edge), f32)
    turn = permutation(edge, 1)
    loads[4].wait()
    loads[5].wait()
    a = split2(t2[...].reshape(xt * edge, t2.shape[2]))
    a_turned = [
        jnp.concatenate([turned(turn, x[l * edge : (l + 1) * edge]) for l in range(xt)], axis=0) for x in a
    ]
    for r in range(0, xt, 2):
        sides = [split2(ints[r + d]) for d in range(2)]
        b = [jnp.concatenate([sides[0][k], sides[1][k]], axis=1) for k in range(2)]
        b_turned = [
            jnp.concatenate([turned(sides[0][k], turn), turned(sides[1][k], turn)], axis=1) for k in range(2)
        ]
        for base, res in ((1, dot3(a, b)), (2 + pairs, dot3(a_turned, b_turned))):
            for l in range(xt):
                for d in range(2):
                    prod[base + l * xt + r + d] = res[l * edge : (l + 1) * edge, d * edge : (d + 1) * edge]
    codes.wait()

    def assemble(c, i):
        lo, half = chunks[c]
        home = cls
        for h in range(levels):
            home = toggle(home, orders[c][h], (i // (1 << h)) % 2)
        ids = []
        for j in range(2 * owned):
            g = (home if j < owned else n_occ - 1 - home) * owned + j % owned
            packed = code_s[g // 128, g % 128]
            base = 0 if j < owned else 1 + pairs
            ids.append([base + (lax.shift_right_logical(packed, width * k) & ((1 << width) - 1)) for k in range(CAP)])
        for at, row in ((0, lo), (half, edge - lo - half)):
            low0, low1, up0, up1 = [
                prod[k[0], row : row + half, :] + prod[k[1], row : row + half, :] + prod[k[2], row : row + half, :]
                for k in ids
            ]
            acc[c][i, 0, at : at + half, :] = low0 + up0
            acc[c][i, 1, at : at + half, :] = low0 + up1
            acc[c][i, 2, at : at + half, :] = low1 + up0

    def step_copy(c, i, h):
        return pltpu.make_async_remote_copy(
            src_ref=acc[c].at[i],
            dst_ref=got[c].at[i],
            send_sem=send_sem.at[c, i],
            recv_sem=recv_sem.at[c, i],
            device_id=(toggle(p, orders[c][h]), q),
            device_id_type=MESH,
        )

    pl.semaphore_wait(barrier, bits + n_vir - 1)

    top = blocks // 2

    @pl.loop(0, top)
    def _(n):
        i = blocks - 1 - n
        for c in early:
            assemble(c, i)
            step_copy(c, i, levels - 1).start()

    flag_copy = pltpu.make_async_remote_copy(
        src_ref=flag, dst_ref=flag_got, send_sem=flag_send, recv_sem=flag_recv,
        device_id=(partner, q), device_id_type=MESH,
    )
    flag_copy.start()

    @pl.loop(0, top)
    def _(n):
        for c in early:
            assemble(c, top - 1 - n)

    @pl.loop(0, blocks)
    def _(n):
        for c in late:
            assemble(c, n)

    for load in loads[6:]:
        load.wait()
    for s in range(owned):
        for b in range(mask.shape[1]):
            rows, cols = pl.ds(s * edge, edge), pl.ds(b * edge, edge)
            hi, lo = split2(lam[rows, cols] * mask[s, b].astype(f32))
            lam_hi[rows, cols] = hi
            lam_lo[rows, cols] = lo

    def ladder(column):
        cols = pl.ds(pl.multiple_of(column * edge, edge), edge)
        return dot3((lam_hi[...], lam_lo[...]), split2(lints[:, cols]))

    lad_copies = []
    for off in range(1, n_vir):
        column = (q + off) % n_vir
        lad[off] = ladder(column)
        lad_copies.append(
            pltpu.make_async_remote_copy(
                src_ref=lad.at[off], dst_ref=lad_got.at[off - 1],
                send_sem=lad_send.at[off - 1], recv_sem=lad_recv.at[off - 1],
                device_id=(p, column), device_id_type=MESH,
            )
        )
        lad_copies[-1].start()
    lad[0] = ladder(q)
    lanes = permutation(edge, upper)

    def add_ladder():
        for copy in lad_copies:
            copy.wait_recv()
        total = lad[0]
        for off in range(1, n_vir):
            total = total + lad_got[off - 1]
        for s in range(owned):
            y = None
            for piece in split3(total[s * edge : (s + 1) * edge]):
                part = dot(lanes, turned(piece, lanes))
                y = part if y is None else y + part
            lad[0, s * edge : (s + 1) * edge, :] = y
        for c in range(CHUNKS):
            lo, half = chunks[c]
            for at, row in ((0, lo), (half, edge - lo - half)):
                here = pl.ds(at, half)
                for j, s in ((0, 0), (1, upper), (2, 1 - upper)):
                    acc[c][0, j, here, :] = acc[c][0, j, here, :] + lad[0, pl.ds(pl.multiple_of(s * edge + row, 8), half), :]

    def take(c, i, h):
        for k in range(h, levels):
            step_copy(c, i + (1 << k), k).wait_recv()
            acc[c][i] = acc[c][i] + got[c][i + (1 << k)]

    def fin_copy(c):
        return pltpu.make_async_remote_copy(
            src_ref=fin[c], dst_ref=fin_got[c], send_sem=fin_send.at[c], recv_sem=fin_recv.at[c],
            device_id=(partner, q), device_id_type=MESH,
        )

    def finish(c):
        m = 2 * chunks[c][1]
        take(c, 0, 0)
        for target, which, swap in ((fin[c], 1 - upper, flag_got), (own[c], upper, flag)):
            keep = jnp.broadcast_to(swap[0:1, :] == 0, (m, edge))
            first, second = acc[c][0, 1 + which], acc[c][0, 2 - which]
            target[0] = jnp.where(keep, acc[c][0, 0], first)
            target[1] = jnp.where(keep, (first - acc[c][0, 0]) + second, second)
            if target is fin[c]:
                fin_copy(c).start()

    for n in range(top):
        for c in late:
            step_copy(c, blocks - 1 - n, levels - 1).start()
        i = top - 1 - n
        if i > 0:
            h = i.bit_length() - 1
            for c in early:
                take(c, i, h + 1)
                step_copy(c, i, h).start()

    add_ladder()
    flag_copy.wait_recv()
    for c in early:
        finish(c)

    for h in reversed(range(levels - 1)):

        @pl.loop(0, 1 << h)
        def _(n):
            i = 2 * (1 << h) - 1 - n
            for c in late:
                take(c, i, h + 1)
                step_copy(c, i, h).start()

    for c in late:
        finish(c)

    for c in range(CHUNKS):
        lo, half = chunks[c]
        size = 2 * owned * half
        rows = permutation(size, upper)
        fin_copy(c).wait_recv()
        y = None
        for piece in split3((own[c][...] + fin_got[c][...]).reshape(size, edge)):
            part = dot(rows, turned(piece, lanes))
            y = part if y is None else y + part
        flips[c][...] = y.reshape(owned, 2 * half, edge)
        for s in range(owned):
            for at, row in ((0, lo), (half, edge - lo - half)):
                out[s * edge + row : s * edge + row + half, :] = flips[c][s + upper * (1 - 2 * s), at : at + half, :]

    flag_copy.wait_send()
    for copy in lad_copies:
        copy.wait_send()
    for c in range(CHUNKS):
        fin_copy(c).wait_send()
        for h in range(levels):

            @pl.loop(1 << h, 2 << h)
            def _(i):
                step_copy(c, i, h).wait_send()


def body(
    n_occ, n_vir,
    t2_tiles, cycle_ints, cycle_left, cycle_right, cycle_dest, lam_ladder, ladder_ints, ladder_mask, partner_slot, denom,
):
    edge = denom.shape[1]
    owned = partner_slot.shape[1]
    xt, kc = cycle_ints.shape[2], cycle_ints.shape[3]
    blocks = n_occ // 2
    chunks = chunk_plan(edge)
    tiles = n_occ * owned
    code_rows = -(-tiles // 128)
    rows = owned * edge
    per_chunk = lambda *lead: tuple(pltpu.VMEM((*lead, 2 * half, edge), f32) for _, half in chunks)
    sem = pltpu.SemaphoreType.DMA
    hbm = pl.BlockSpec(memory_space=pltpu.HBM)
    smem = lambda x: pltpu.SMEM(x.shape, x.dtype)
    sym = pl.pallas_call(
        functools.partial(kernel, n_occ, n_vir, chunks),
        out_shape=pltpu.VMEM((rows, edge), f32),
        in_specs=[hbm] * 9,
        out_specs=pl.BlockSpec(memory_space=pltpu.VMEM),
        scratch_shapes=[
            smem(cycle_left),
            smem(cycle_right),
            smem(cycle_dest),
            smem(ladder_mask),
            smem(partner_slot),
            pltpu.VMEM((xt, edge, kc), f32),
            pltpu.VMEM((xt, kc, edge), f32),
            pltpu.VMEM(lam_ladder.shape, f32),
            pltpu.VMEM(ladder_ints.shape, f32),
            pltpu.VMEM((code_rows, 128), jnp.int32),
            pltpu.SMEM((code_rows, 128), jnp.int32),
            pltpu.VMEM((2 + 2 * xt * xt, edge, edge), f32),
            pltpu.VMEM(lam_ladder.shape, bf16),
            pltpu.VMEM(lam_ladder.shape, bf16),
            pltpu.VMEM((n_vir, rows, edge), f32),
            pltpu.VMEM((n_vir - 1, rows, edge), f32),
            pltpu.VMEM((8, 128), jnp.int32),
            pltpu.VMEM((8, 128), jnp.int32),
            (
                per_chunk(blocks, 3), per_chunk(blocks, 3),
                per_chunk(owned), per_chunk(owned), per_chunk(owned), per_chunk(owned),
            ),
            sem((9,)),
            sem,
            sem((CHUNKS, blocks)),
            sem((CHUNKS, blocks)),
            sem((CHUNKS,)),
            sem((CHUNKS,)),
            sem((n_vir - 1,)),
            sem((n_vir - 1,)),
            sem,
            sem,
        ],
        compiler_params=pltpu.CompilerParams(
            collective_id=0, has_side_effects=True, vmem_limit_bytes=56 * 1024 * 1024
        ),
        cost_estimate=pl.CostEstimate(flops=10**9, bytes_accessed=4 * 10**6, transcendentals=0),
    )(cycle_left, cycle_right, cycle_dest, ladder_mask, partner_slot, t2_tiles, cycle_ints, lam_ladder, ladder_ints)
    return sym / denom


def solution(mesh):
    in_specs = (
        P("occ", "vir", None, None, None),
        P("occ", "vir", None, None, None),
        P("occ", "vir", None),
        P("occ", "vir", None),
        P("occ", "vir", None),
        P("occ", "vir"),
        P("vir", None),
        P("occ", "vir"),
        P("occ", None),
        P("occ", "vir"),
    )
    local = functools.partial(body, mesh.shape["occ"], mesh.shape["vir"])
    return jax.shard_map(local, mesh=mesh, in_specs=in_specs, out_specs=P("occ", "vir"), check_vma=False)
```

```python
import functools

import jax
import jax.numpy as jnp
from jax import lax
from jax.experimental import pallas as pl
from jax.experimental.pallas import tpu as pltpu
from jax.sharding import PartitionSpec as P

CAP = 3
MESH = pl.DeviceIdType.MESH
f32 = jnp.float32
bf16 = jnp.bfloat16


def split2(x):
    hi = x.astype(bf16)
    return hi, (x - hi.astype(f32)).astype(bf16)


def dot(a, b):
    return jnp.dot(a, b, preferred_element_type=f32)


def dot3(a, b):
    return dot(a[0], b[0]) + (dot(a[0], b[1]) + dot(a[1], b[0]))


CHUNKS = 3


def chunk_plan(edge):
    sizes = [units * (edge // 16) for units in (3, 3, 2)]
    return [(sum(sizes[:c]), sizes[c]) for c in range(CHUNKS)]


def turned(matrix, x):
    return dot(matrix, x).astype(bf16)


def split3(x):
    hi, rest = split2(x)
    mid, low = split2(x - hi.astype(f32))
    return hi, mid, low


def permutation(size, reverse):
    row = lax.broadcasted_iota(jnp.int32, (size, size), 0)
    col = lax.broadcasted_iota(jnp.int32, (size, size), 1)
    target = row + reverse * (size - 1 - 2 * row)
    return jnp.where(target == col, 1.0, 0.0).astype(bf16)


def kernel(
    n_occ, n_vir, chunks,
    left_hbm, right_hbm, dest_hbm, mask_hbm, slot_hbm, t2_hbm, ints_hbm, lam_hbm, lints_hbm,
    out,
    left, right, dest, mask, slot,
    t2, ints, lam, lints, code_v, code_s, prod, lam_hi, lam_lo, lad, lad_got, flag, flag_got,
    per_chunk,
    load_sem, code_sem, send_sem, recv_sem, fin_send, fin_recv, lad_send, lad_recv, flag_send, flag_recv,
):
    acc, got, own, fin, fin_got, flips = per_chunk
    edge = prod.shape[1]
    xt = t2.shape[0]
    pairs = xt * xt
    owned = 2
    count = dest.shape[2]
    bits = n_occ.bit_length() - 1
    levels = bits - 1
    blocks = n_occ // 2
    width = pairs.bit_length()
    p = lax.axis_index("occ")
    q = lax.axis_index("vir")
    upper = lax.div(p, blocks)
    cls = p + upper * (n_occ - 1 - 2 * p)
    partner = n_occ - 1 - p
    orders = [[1 << ((c + levels - 1 - h) % levels) for h in range(levels)] for c in range(CHUNKS)]
    offsets = {1 << b: (1 << b) * (1 - 2 * lax.rem(lax.div(p, 1 << b), 2)) for b in range(levels)}
    peers = {bit: p + offset for bit, offset in offsets.items()}
    turns = {bit: offset * (1 - 2 * upper) for bit, offset in offsets.items()}

    loads = [
        pltpu.make_async_copy(src, dst, load_sem.at[i])
        for i, (src, dst) in enumerate(
            (
                (left_hbm, left), (right_hbm, right), (dest_hbm, dest), (slot_hbm, slot),
                (t2_hbm.at[0, 0], t2), (ints_hbm.at[0, 0], ints),
                (mask_hbm, mask), (lam_hbm, lam), (lints_hbm, lints),
            )
        )
    ]
    for load in loads:
        load.start()

    barrier = pltpu.get_barrier_semaphore()
    for peer in peers.values():
        pl.semaphore_signal(barrier, inc=1, device_id=(peer, q), device_id_type=MESH)
    pl.semaphore_signal(barrier, inc=1, device_id=(partner, q), device_id_type=MESH)
    for off in range(1, n_vir):
        pl.semaphore_signal(barrier, inc=1, device_id=(p, lax.rem(q + off, n_vir)), device_id_type=MESH)

    tile_id = lax.broadcasted_iota(jnp.int32, code_v.shape, 0) * 128 + lax.broadcasted_iota(
        jnp.int32, code_v.shape, 1
    )
    for load in loads[:4]:
        load.wait()

    def note(t, packed):
        code = left[0, 0, t] * xt + right[0, 0, t] + 1
        return jnp.where(tile_id == dest[0, 0, t], packed * (1 << width) + code, packed)

    code_v[...] = lax.fori_loop(0, count, note, jnp.zeros(code_v.shape, jnp.int32), unroll=8)
    codes = pltpu.make_async_copy(code_v, code_s, code_sem)
    codes.start()
    flag[...] = jnp.full(flag.shape, slot[0, 0], jnp.int32)

    prod[0] = jnp.zeros((edge, edge), f32)
    prod[1 + pairs] = jnp.zeros((edge, edge), f32)
    turn = permutation(edge, 1)
    loads[4].wait()
    loads[5].wait()
    a = split2(t2[...].reshape(xt * edge, t2.shape[2]))
    a_turned = [
        jnp.concatenate([turned(turn, x[l * edge : (l + 1) * edge]) for l in range(xt)], axis=0) for x in a
    ]
    for r in range(0, xt, 2):
        sides = [split2(ints[r + d]) for d in range(2)]
        b = [jnp.concatenate([sides[0][k], sides[1][k]], axis=1) for k in range(2)]
        b_turned = [
            jnp.concatenate([turned(sides[0][k], turn), turned(sides[1][k], turn)], axis=1) for k in range(2)
        ]
        for base, res in ((1, dot3(a, b)), (2 + pairs, dot3(a_turned, b_turned))):
            for l in range(xt):
                for d in range(2):
                    prod[base + l * xt + r + d] = res[l * edge : (l + 1) * edge, d * edge : (d + 1) * edge]
    codes.wait()

    def place(c, rel):
        return sum(1 << h for h in range(levels) if rel & orders[c][h])

    def assemble(rel):
        home = cls
        for bit in turns:
            if rel & bit:
                home = home + turns[bit]
        ids = []
        for j in range(2 * owned):
            g = (home if j < owned else n_occ - 1 - home) * owned + j % owned
            packed = code_s[0, g] if code_s.shape[0] == 1 else code_s[lax.div(g, 128), lax.rem(g, 128)]
            base = 0 if j < owned else 1 + pairs
            ids.append([base + (lax.shift_right_logical(packed, width * k) & ((1 << width) - 1)) for k in range(CAP)])
        for c in range(CHUNKS):
            lo, half = chunks[c]
            i = place(c, rel)
            for at, row in ((0, lo), (half, edge - lo - half)):
                low0, low1, up0, up1 = [
                    prod[k[0], row : row + half, :] + prod[k[1], row : row + half, :] + prod[k[2], row : row + half, :]
                    for k in ids
                ]
                acc[c][i, 0, at : at + half, :] = low0 + up0
                acc[c][i, 1, at : at + half, :] = low0 + up1
                acc[c][i, 2, at : at + half, :] = low1 + up0
            if i >= blocks // 2:
                step_copy(c, i, levels - 1).start()

    def step_copy(c, i, h):
        return pltpu.make_async_remote_copy(
            src_ref=acc[c].at[i],
            dst_ref=got[c].at[i],
            send_sem=send_sem.at[c, i],
            recv_sem=recv_sem.at[c, i],
            device_id=(peers[orders[c][h]], q),
            device_id_type=MESH,
        )

    pl.semaphore_wait(barrier, bits + n_vir - 1)

    for rel in sorted(range(blocks), key=lambda r: -sum(r >> b & 1 for b in range(levels))):
        assemble(rel)

    flag_copy = pltpu.make_async_remote_copy(
        src_ref=flag, dst_ref=flag_got, send_sem=flag_send, recv_sem=flag_recv,
        device_id=(partner, q), device_id_type=MESH,
    )
    flag_copy.start()

    for load in loads[6:]:
        load.wait()
    for s in range(owned):
        for b in range(mask.shape[1]):
            rows, cols = pl.ds(s * edge, edge), pl.ds(b * edge, edge)
            hi, lo = split2(lam[rows, cols] * mask[s, b].astype(f32))
            lam_hi[rows, cols] = hi
            lam_lo[rows, cols] = lo

    def ladder(column):
        cols = pl.ds(pl.multiple_of(column * edge, edge), edge)
        return dot3((lam_hi[...], lam_lo[...]), split2(lints[:, cols]))

    lad_copies = []
    for off in range(1, n_vir):
        column = lax.rem(q + off, n_vir)
        lad[off] = ladder(column)
        lad_copies.append(
            pltpu.make_async_remote_copy(
                src_ref=lad.at[off], dst_ref=lad_got.at[off - 1],
                send_sem=lad_send.at[off - 1], recv_sem=lad_recv.at[off - 1],
                device_id=(p, column), device_id_type=MESH,
            )
        )
        lad_copies[-1].start()
    lad[0] = ladder(q)
    lanes = permutation(edge, upper)

    def add_ladder():
        for copy in lad_copies:
            copy.wait_recv()
        total = lad[0]
        for off in range(1, n_vir):
            total = total + lad_got[off - 1]
        for s in range(owned):
            y = None
            for piece in split3(total[s * edge : (s + 1) * edge]):
                part = dot(lanes, turned(piece, lanes))
                y = part if y is None else y + part
            lad[0, s * edge : (s + 1) * edge, :] = y
        for c in range(CHUNKS):
            lo, half = chunks[c]
            for at, row in ((0, lo), (half, edge - lo - half)):
                here = pl.ds(at, half)
                for j, s in ((0, 0), (1, upper), (2, 1 - upper)):
                    acc[c][0, j, here, :] = acc[c][0, j, here, :] + lad[0, pl.ds(pl.multiple_of(s * edge + row, 8), half), :]

    def take(c, i, h):
        for k in range(h, levels):
            step_copy(c, i + (1 << k), k).wait_recv()
            acc[c][i] = acc[c][i] + got[c][i + (1 << k)]

    def fin_copy(c):
        return pltpu.make_async_remote_copy(
            src_ref=fin[c], dst_ref=fin_got[c], send_sem=fin_send.at[c], recv_sem=fin_recv.at[c],
            device_id=(partner, q), device_id_type=MESH,
        )

    def finish(c):
        m = 2 * chunks[c][1]
        take(c, 0, 0)
        for target, which, swap in ((fin[c], 1 - upper, flag_got), (own[c], upper, flag)):
            keep = jnp.broadcast_to(swap[0:1, :] == 0, (m, edge))
            first, second = acc[c][0, 1 + which], acc[c][0, 2 - which]
            target[0] = jnp.where(keep, acc[c][0, 0], first)
            target[1] = jnp.where(keep, (first - acc[c][0, 0]) + second, second)
            if target is fin[c]:
                fin_copy(c).start()

    for h in reversed(range(levels - 1)):
        if h == 0:
            add_ladder()
        for i in reversed(range(1 << h, 2 << h)):
            for c in range(CHUNKS):
                take(c, i, h + 1)
                step_copy(c, i, h).start()

    flag_copy.wait_recv()
    for c in range(CHUNKS):
        finish(c)

    for c in range(CHUNKS):
        lo, half = chunks[c]
        size = 2 * owned * half
        rows = permutation(size, upper)
        fin_copy(c).wait_recv()
        y = None
        for piece in split3((own[c][...] + fin_got[c][...]).reshape(size, edge)):
            part = dot(rows, turned(piece, lanes))
            y = part if y is None else y + part
        flips[c][...] = y.reshape(owned, 2 * half, edge)
        for s in range(owned):
            for at, row in ((0, lo), (half, edge - lo - half)):
                out[s * edge + row : s * edge + row + half, :] = flips[c][s + upper * (1 - 2 * s), at : at + half, :]

    flag_copy.wait_send()
    for copy in lad_copies:
        copy.wait_send()
    for c in range(CHUNKS):
        fin_copy(c).wait_send()
        for h in range(levels):

            @pl.loop(1 << h, 2 << h)
            def _(i):
                step_copy(c, i, h).wait_send()


def body(
    n_occ, n_vir,
    t2_tiles, cycle_ints, cycle_left, cycle_right, cycle_dest, lam_ladder, ladder_ints, ladder_mask, partner_slot, denom,
):
    edge = denom.shape[1]
    owned = partner_slot.shape[1]
    xt, kc = cycle_ints.shape[2], cycle_ints.shape[3]
    blocks = n_occ // 2
    chunks = chunk_plan(edge)
    tiles = n_occ * owned
    code_rows = -(-tiles // 128)
    rows = owned * edge
    per_chunk = lambda *lead: tuple(pltpu.VMEM((*lead, 2 * half, edge), f32) for _, half in chunks)
    sem = pltpu.SemaphoreType.DMA
    hbm = pl.BlockSpec(memory_space=pltpu.HBM)
    smem = lambda x: pltpu.SMEM(x.shape, x.dtype)
    sym = pl.pallas_call(
        functools.partial(kernel, n_occ, n_vir, chunks),
        out_shape=pltpu.VMEM((rows, edge), f32),
        in_specs=[hbm] * 9,
        out_specs=pl.BlockSpec(memory_space=pltpu.VMEM),
        scratch_shapes=[
            smem(cycle_left),
            smem(cycle_right),
            smem(cycle_dest),
            smem(ladder_mask),
            smem(partner_slot),
            pltpu.VMEM((xt, edge, kc), f32),
            pltpu.VMEM((xt, kc, edge), f32),
            pltpu.VMEM(lam_ladder.shape, f32),
            pltpu.VMEM(ladder_ints.shape, f32),
            pltpu.VMEM((code_rows, 128), jnp.int32),
            pltpu.SMEM((code_rows, 128), jnp.int32),
            pltpu.VMEM((2 + 2 * xt * xt, edge, edge), f32),
            pltpu.VMEM(lam_ladder.shape, bf16),
            pltpu.VMEM(lam_ladder.shape, bf16),
            pltpu.VMEM((n_vir, rows, edge), f32),
            pltpu.VMEM((n_vir - 1, rows, edge), f32),
            pltpu.VMEM((8, 128), jnp.int32),
            pltpu.VMEM((8, 128), jnp.int32),
            (
                per_chunk(blocks, 3), per_chunk(blocks, 3),
                per_chunk(owned), per_chunk(owned), per_chunk(owned), per_chunk(owned),
            ),
            sem((9,)),
            sem,
            sem((CHUNKS, blocks)),
            sem((CHUNKS, blocks)),
            sem((CHUNKS,)),
            sem((CHUNKS,)),
            sem((n_vir - 1,)),
            sem((n_vir - 1,)),
            sem,
            sem,
        ],
        compiler_params=pltpu.CompilerParams(
            collective_id=0, has_side_effects=True, vmem_limit_bytes=56 * 1024 * 1024
        ),
        cost_estimate=pl.CostEstimate(flops=10**9, bytes_accessed=4 * 10**6, transcendentals=0),
    )(cycle_left, cycle_right, cycle_dest, ladder_mask, partner_slot, t2_tiles, cycle_ints, lam_ladder, ladder_ints)
    return sym / denom


def solution(mesh):
    in_specs = (
        P("occ", "vir", None, None, None),
        P("occ", "vir", None, None, None),
        P("occ", "vir", None),
        P("occ", "vir", None),
        P("occ", "vir", None),
        P("occ", "vir"),
        P("vir", None),
        P("occ", "vir"),
        P("occ", None),
        P("occ", "vir"),
    )
    local = functools.partial(body, mesh.shape["occ"], mesh.shape["vir"])
    return jax.shard_map(local, mesh=mesh, in_specs=in_specs, out_specs=P("occ", "vir"), check_vma=False)
```

```python
import functools

import jax
import jax.numpy as jnp
from jax import lax
from jax.experimental import pallas as pl
from jax.experimental.pallas import tpu as pltpu
from jax.sharding import PartitionSpec as P

CAP = 3
MESH = pl.DeviceIdType.MESH
f32 = jnp.float32
bf16 = jnp.bfloat16


def split2(x):
    hi = x.astype(bf16)
    return hi, (x - hi.astype(f32)).astype(bf16)


def dot(a, b):
    return jnp.dot(a, b, preferred_element_type=f32)


def dot3(a, b):
    return dot(a[0], b[0]) + (dot(a[0], b[1]) + dot(a[1], b[0]))


CHUNKS = 6
AXES = 3


def chunk_plan(edge):
    sizes = [units * (edge // 16) for units in (2, 2, 1, 1, 1, 1)]
    return [(sum(sizes[:c]), sizes[c]) for c in range(CHUNKS)]


def turned(matrix, x):
    return dot(matrix, x).astype(bf16)


def split3(x):
    hi, rest = split2(x)
    mid, low = split2(x - hi.astype(f32))
    return hi, mid, low


def permutation(size, reverse):
    row = lax.broadcasted_iota(jnp.int32, (size, size), 0)
    col = lax.broadcasted_iota(jnp.int32, (size, size), 1)
    target = row + reverse * (size - 1 - 2 * row)
    return jnp.where(target == col, 1.0, 0.0).astype(bf16)


def kernel(
    n_occ, n_vir, chunks,
    left_hbm, right_hbm, dest_hbm, mask_hbm, slot_hbm, t2_hbm, ints_hbm, lam_hbm, lints_hbm,
    out,
    left, right, dest, mask, slot,
    t2, ints, lam, lints, code_v, code_s, prod, lam_hi, lam_lo, lad, lad_got, flag, flag_got,
    per_chunk,
    load_sem, code_sem, send_sem, recv_sem, fin_send, fin_recv, lad_send, lad_recv, flag_send, flag_recv,
):
    acc, got, own, fin, fin_got, flips = per_chunk
    edge = prod.shape[1]
    xt = t2.shape[0]
    pairs = xt * xt
    owned = 2
    count = dest.shape[2]
    bits = n_occ.bit_length() - 1
    levels = bits - 1
    blocks = n_occ // 2
    width = pairs.bit_length()
    p = lax.axis_index("occ")
    q = lax.axis_index("vir")
    upper = lax.div(p, blocks)
    cls = p + upper * (n_occ - 1 - 2 * p)
    partner = n_occ - 1 - p
    orders = [[1 << ((c % AXES + levels - 1 - h) % levels) for h in range(levels)] for c in range(CHUNKS)]
    early, late = range(AXES), range(AXES, CHUNKS)
    low, high = levels - 1, levels
    pieces = [(1 << h, 2 << h, h) for h in range(levels - 1)]
    pieces += [(blocks // 2, 3 * blocks // 4, levels - 1), (3 * blocks // 4, blocks, levels - 1)]
    offsets = {1 << b: (1 << b) * (1 - 2 * lax.rem(lax.div(p, 1 << b), 2)) for b in range(levels)}
    peers = {bit: p + offset for bit, offset in offsets.items()}
    turns = {bit: offset * (1 - 2 * upper) for bit, offset in offsets.items()}

    loads = [
        pltpu.make_async_copy(src, dst, load_sem.at[i])
        for i, (src, dst) in enumerate(
            (
                (left_hbm, left), (right_hbm, right), (dest_hbm, dest), (slot_hbm, slot),
                (t2_hbm.at[0, 0], t2), (ints_hbm.at[0, 0], ints),
                (mask_hbm, mask), (lam_hbm, lam), (lints_hbm, lints),
            )
        )
    ]
    for load in loads:
        load.start()

    barrier = pltpu.get_barrier_semaphore()
    for peer in peers.values():
        pl.semaphore_signal(barrier, inc=1, device_id=(peer, q), device_id_type=MESH)
    pl.semaphore_signal(barrier, inc=1, device_id=(partner, q), device_id_type=MESH)
    for off in range(1, n_vir):
        pl.semaphore_signal(barrier, inc=1, device_id=(p, lax.rem(q + off, n_vir)), device_id_type=MESH)

    tile_id = lax.broadcasted_iota(jnp.int32, code_v.shape, 0) * 128 + lax.broadcasted_iota(
        jnp.int32, code_v.shape, 1
    )
    for load in loads[:4]:
        load.wait()

    def note(t, packed):
        code = left[0, 0, t] * xt + right[0, 0, t] + 1
        return jnp.where(tile_id == dest[0, 0, t], packed * (1 << width) + code, packed)

    code_v[...] = lax.fori_loop(0, count, note, jnp.zeros(code_v.shape, jnp.int32), unroll=8)
    codes = pltpu.make_async_copy(code_v, code_s, code_sem)
    codes.start()
    flag[...] = jnp.full(flag.shape, slot[0, 0], jnp.int32)

    prod[0] = jnp.zeros((edge, edge), f32)
    prod[1 + pairs] = jnp.zeros((edge, edge), f32)
    turn = permutation(edge, 1)
    loads[4].wait()
    loads[5].wait()
    a = split2(t2[...].reshape(xt * edge, t2.shape[2]))
    a_turned = [
        jnp.concatenate([turned(turn, x[l * edge : (l + 1) * edge]) for l in range(xt)], axis=0) for x in a
    ]
    for r in range(0, xt, 2):
        sides = [split2(ints[r + d]) for d in range(2)]
        b = [jnp.concatenate([sides[0][k], sides[1][k]], axis=1) for k in range(2)]
        b_turned = [
            jnp.concatenate([turned(sides[0][k], turn), turned(sides[1][k], turn)], axis=1) for k in range(2)
        ]
        for base, res in ((1, dot3(a, b)), (2 + pairs, dot3(a_turned, b_turned))):
            for l in range(xt):
                for d in range(2):
                    prod[base + l * xt + r + d] = res[l * edge : (l + 1) * edge, d * edge : (d + 1) * edge]
    codes.wait()

    def place(c, rel):
        return sum(1 << h for h in range(levels) if rel & orders[c][h])

    def assemble(rel):
        home = cls
        for bit in turns:
            if rel & bit:
                home = home + turns[bit]
        ids = []
        for j in range(2 * owned):
            g = (home if j < owned else n_occ - 1 - home) * owned + j % owned
            packed = code_s[0, g] if code_s.shape[0] == 1 else code_s[lax.div(g, 128), lax.rem(g, 128)]
            base = 0 if j < owned else 1 + pairs
            ids.append([base + (lax.shift_right_logical(packed, width * k) & ((1 << width) - 1)) for k in range(CAP)])
        for c in range(CHUNKS):
            lo, half = chunks[c]
            i = place(c, rel)
            for at, row in ((0, lo), (half, edge - lo - half)):
                low0, low1, up0, up1 = [
                    prod[k[0], row : row + half, :] + prod[k[1], row : row + half, :] + prod[k[2], row : row + half, :]
                    for k in ids
                ]
                acc[c][i, 0, at : at + half, :] = low0 + up0
                acc[c][i, 1, at : at + half, :] = low0 + up1
                acc[c][i, 2, at : at + half, :] = low1 + up0

    def step_copy(c, n):
        start, stop, h = pieces[n]
        return pltpu.make_async_remote_copy(
            src_ref=acc[c].at[pl.ds(start, stop - start)],
            dst_ref=got[c].at[pl.ds(start, stop - start)],
            send_sem=send_sem.at[c, n],
            recv_sem=recv_sem.at[c, n],
            device_id=(peers[orders[c][h]], q),
            device_id_type=MESH,
        )

    pl.semaphore_wait(barrier, bits + n_vir - 1)

    rels = sorted(range(blocks), key=lambda r: -sum(r >> b & 1 for b in range(levels)))
    done, sent = set(), set()
    for rel in rels:
        assemble(rel)
        done.add(rel)
        for n, group in ((high, early), (low, early), (high, late), (low, late)):
            start, stop, _ = pieces[n]
            held = [r for r in range(blocks) for c in group if start <= place(c, r) < stop]
            if (n, group) not in sent and done.issuperset(held) and (group is early or (low, early) in sent):
                sent.add((n, group))
                for c in group:
                    step_copy(c, n).start()

    flag_copy = pltpu.make_async_remote_copy(
        src_ref=flag, dst_ref=flag_got, send_sem=flag_send, recv_sem=flag_recv,
        device_id=(partner, q), device_id_type=MESH,
    )
    flag_copy.start()

    for load in loads[6:]:
        load.wait()
    for s in range(owned):
        for b in range(mask.shape[1]):
            rows, cols = pl.ds(s * edge, edge), pl.ds(b * edge, edge)
            hi, lo = split2(lam[rows, cols] * mask[s, b].astype(f32))
            lam_hi[rows, cols] = hi
            lam_lo[rows, cols] = lo

    def ladder(column):
        cols = pl.ds(pl.multiple_of(column * edge, edge), edge)
        return dot3((lam_hi[...], lam_lo[...]), split2(lints[:, cols]))

    lad_copies = []
    for off in range(1, n_vir):
        column = lax.rem(q + off, n_vir)
        lad[off] = ladder(column)
        lad_copies.append(
            pltpu.make_async_remote_copy(
                src_ref=lad.at[off], dst_ref=lad_got.at[off - 1],
                send_sem=lad_send.at[off - 1], recv_sem=lad_recv.at[off - 1],
                device_id=(p, column), device_id_type=MESH,
            )
        )
        lad_copies[-1].start()
    lad[0] = ladder(q)
    lanes = permutation(edge, upper)

    def add_ladder():
        for copy in lad_copies:
            copy.wait_recv()
        total = lad[0]
        for off in range(1, n_vir):
            total = total + lad_got[off - 1]
        for s in range(owned):
            y = None
            for piece in split3(total[s * edge : (s + 1) * edge]):
                part = dot(lanes, turned(piece, lanes))
                y = part if y is None else y + part
            lad[0, s * edge : (s + 1) * edge, :] = y
        for c in range(CHUNKS):
            lo, half = chunks[c]
            for at, row in ((0, lo), (half, edge - lo - half)):
                here = pl.ds(at, half)
                for j, s in ((0, 0), (1, upper), (2, 1 - upper)):
                    acc[c][0, j, here, :] = acc[c][0, j, here, :] + lad[0, pl.ds(pl.multiple_of(s * edge + row, 8), half), :]

    arrived = set()

    def take(c, start, stop):
        for k in reversed(range(levels)):
            if 1 << k < stop:
                continue
            n = k if k < low else high if start >= blocks // 4 else low
            if (c, n) not in arrived:
                arrived.add((c, n))
                step_copy(c, n).wait_recv()
            acc[c][start:stop] = acc[c][start:stop] + got[c][start + (1 << k) : stop + (1 << k)]

    def fin_copy(c):
        return pltpu.make_async_remote_copy(
            src_ref=fin[c], dst_ref=fin_got[c], send_sem=fin_send.at[c], recv_sem=fin_recv.at[c],
            device_id=(partner, q), device_id_type=MESH,
        )

    def finish(c):
        m = 2 * chunks[c][1]
        take(c, 0, 1)
        for target, which, swap in ((fin[c], 1 - upper, flag_got), (own[c], upper, flag)):
            keep = jnp.broadcast_to(swap[0:1, :] == 0, (m, edge))
            first, second = acc[c][0, 1 + which], acc[c][0, 2 - which]
            target[0] = jnp.where(keep, acc[c][0, 0], first)
            target[1] = jnp.where(keep, (first - acc[c][0, 0]) + second, second)
            if target is fin[c]:
                fin_copy(c).start()

    for group in (early, late):
        for h in reversed(range(levels - 1)):
            for c in group:
                take(c, 1 << h, 2 << h)
                step_copy(c, h).start()
        if group is early:
            add_ladder()
            flag_copy.wait_recv()
        for c in group:
            finish(c)

    for c in range(CHUNKS):
        lo, half = chunks[c]
        size = 2 * owned * half
        rows = permutation(size, upper)
        fin_copy(c).wait_recv()
        y = None
        for piece in split3((own[c][...] + fin_got[c][...]).reshape(size, edge)):
            part = dot(rows, turned(piece, lanes))
            y = part if y is None else y + part
        flips[c][...] = y.reshape(owned, 2 * half, edge)
        for s in range(owned):
            for at, row in ((0, lo), (half, edge - lo - half)):
                out[s * edge + row : s * edge + row + half, :] = flips[c][s + upper * (1 - 2 * s), at : at + half, :]

    flag_copy.wait_send()
    for copy in lad_copies:
        copy.wait_send()
    for c in range(CHUNKS):
        fin_copy(c).wait_send()
        for n in range(len(pieces)):
            step_copy(c, n).wait_send()


def body(
    n_occ, n_vir,
    t2_tiles, cycle_ints, cycle_left, cycle_right, cycle_dest, lam_ladder, ladder_ints, ladder_mask, partner_slot, denom,
):
    edge = denom.shape[1]
    owned = partner_slot.shape[1]
    xt, kc = cycle_ints.shape[2], cycle_ints.shape[3]
    blocks = n_occ // 2
    chunks = chunk_plan(edge)
    tiles = n_occ * owned
    code_rows = -(-tiles // 128)
    rows = owned * edge
    per_chunk = lambda *lead: tuple(pltpu.VMEM((*lead, 2 * half, edge), f32) for _, half in chunks)
    sem = pltpu.SemaphoreType.DMA
    hbm = pl.BlockSpec(memory_space=pltpu.HBM)
    smem = lambda x: pltpu.SMEM(x.shape, x.dtype)
    sym = pl.pallas_call(
        functools.partial(kernel, n_occ, n_vir, chunks),
        out_shape=pltpu.VMEM((rows, edge), f32),
        in_specs=[hbm] * 9,
        out_specs=pl.BlockSpec(memory_space=pltpu.VMEM),
        scratch_shapes=[
            smem(cycle_left),
            smem(cycle_right),
            smem(cycle_dest),
            smem(ladder_mask),
            smem(partner_slot),
            pltpu.VMEM((xt, edge, kc), f32),
            pltpu.VMEM((xt, kc, edge), f32),
            pltpu.VMEM(lam_ladder.shape, f32),
            pltpu.VMEM(ladder_ints.shape, f32),
            pltpu.VMEM((code_rows, 128), jnp.int32),
            pltpu.SMEM((code_rows, 128), jnp.int32),
            pltpu.VMEM((2 + 2 * xt * xt, edge, edge), f32),
            pltpu.VMEM(lam_ladder.shape, bf16),
            pltpu.VMEM(lam_ladder.shape, bf16),
            pltpu.VMEM((n_vir, rows, edge), f32),
            pltpu.VMEM((n_vir - 1, rows, edge), f32),
            pltpu.VMEM((8, 128), jnp.int32),
            pltpu.VMEM((8, 128), jnp.int32),
            (
                per_chunk(blocks, 3), per_chunk(blocks, 3),
                per_chunk(owned), per_chunk(owned), per_chunk(owned), per_chunk(owned),
            ),
            sem((9,)),
            sem,
            sem((CHUNKS, n_occ.bit_length())),
            sem((CHUNKS, n_occ.bit_length())),
            sem((CHUNKS,)),
            sem((CHUNKS,)),
            sem((n_vir - 1,)),
            sem((n_vir - 1,)),
            sem,
            sem,
        ],
        compiler_params=pltpu.CompilerParams(
            collective_id=0, has_side_effects=True, vmem_limit_bytes=56 * 1024 * 1024
        ),
        cost_estimate=pl.CostEstimate(flops=10**9, bytes_accessed=4 * 10**6, transcendentals=0),
    )(cycle_left, cycle_right, cycle_dest, ladder_mask, partner_slot, t2_tiles, cycle_ints, lam_ladder, ladder_ints)
    return sym / denom


def solution(mesh):
    in_specs = (
        P("occ", "vir", None, None, None),
        P("occ", "vir", None, None, None),
        P("occ", "vir", None),
        P("occ", "vir", None),
        P("occ", "vir", None),
        P("occ", "vir"),
        P("vir", None),
        P("occ", "vir"),
        P("occ", None),
        P("occ", "vir"),
    )
    local = functools.partial(body, mesh.shape["occ"], mesh.shape["vir"])
    return jax.shard_map(local, mesh=mesh, in_specs=in_specs, out_specs=P("occ", "vir"), check_vma=False)
```

```python
import functools

import jax
import jax.numpy as jnp
from jax import lax
from jax.experimental import pallas as pl
from jax.experimental.pallas import tpu as pltpu
from jax.sharding import PartitionSpec as P

CAP = 3
MESH = pl.DeviceIdType.MESH
f32 = jnp.float32
bf16 = jnp.bfloat16


def split2(x):
    hi = x.astype(bf16)
    return hi, (x - hi.astype(f32)).astype(bf16)


def dot(a, b):
    return jnp.dot(a, b, preferred_element_type=f32)


def dot3(a, b):
    return dot(a[0], b[0]) + (dot(a[0], b[1]) + dot(a[1], b[0]))


CHUNKS = 3


def chunk_plan(edge):
    sizes = [units * (edge // 16) for units in (3, 3, 2)]
    return [(sum(sizes[:c]), sizes[c]) for c in range(CHUNKS)]


def turned(matrix, x):
    return dot(matrix, x).astype(bf16)


def split3(x):
    hi, rest = split2(x)
    mid, low = split2(x - hi.astype(f32))
    return hi, mid, low


def permutation(size, reverse):
    row = lax.broadcasted_iota(jnp.int32, (size, size), 0)
    col = lax.broadcasted_iota(jnp.int32, (size, size), 1)
    target = row + reverse * (size - 1 - 2 * row)
    return jnp.where(target == col, 1.0, 0.0).astype(bf16)


def kernel(
    n_occ, n_vir, chunks,
    left_hbm, right_hbm, dest_hbm, mask_hbm, slot_hbm, t2_hbm, ints_hbm, lam_hbm, lints_hbm,
    out,
    left, right, dest, mask, slot,
    t2, ints, lam, lints, code_v, code_s, prod, lam_hi, lam_lo, lad, lad_got, flag, flag_got,
    per_chunk,
    load_sem, code_sem, send_sem, recv_sem, fin_send, fin_recv, lad_send, lad_recv, flag_send, flag_recv,
):
    acc, got, own, fin, fin_got = per_chunk
    edge = prod.shape[1]
    xt = t2.shape[0]
    pairs = xt * xt
    owned = 2
    count = dest.shape[2]
    bits = n_occ.bit_length() - 1
    levels = bits - 1
    blocks = n_occ // 2
    width = pairs.bit_length()
    p = lax.axis_index("occ")
    q = lax.axis_index("vir")
    upper = lax.div(p, blocks)
    cls = p + upper * (n_occ - 1 - 2 * p)
    partner = n_occ - 1 - p
    orders = [[1 << ((c + levels - 1 - h) % levels) for h in range(levels)] for c in range(CHUNKS)]
    offsets = {1 << b: (1 << b) * (1 - 2 * lax.rem(lax.div(p, 1 << b), 2)) for b in range(levels)}
    peers = {bit: p + offset for bit, offset in offsets.items()}
    turns = {bit: offset * (1 - 2 * upper) for bit, offset in offsets.items()}

    loads = [
        pltpu.make_async_copy(src, dst, load_sem.at[i])
        for i, (src, dst) in enumerate(
            (
                (left_hbm, left), (right_hbm, right), (dest_hbm, dest), (slot_hbm, slot),
                (t2_hbm.at[0, 0], t2), (ints_hbm.at[0, 0], ints),
                (mask_hbm, mask), (lam_hbm, lam), (lints_hbm, lints),
            )
        )
    ]
    for load in loads:
        load.start()

    barrier = pltpu.get_barrier_semaphore()
    for peer in peers.values():
        pl.semaphore_signal(barrier, inc=1, device_id=(peer, q), device_id_type=MESH)
    pl.semaphore_signal(barrier, inc=1, device_id=(partner, q), device_id_type=MESH)
    for off in range(1, n_vir):
        pl.semaphore_signal(barrier, inc=1, device_id=(p, lax.rem(q + off, n_vir)), device_id_type=MESH)

    tile_id = lax.broadcasted_iota(jnp.int32, code_v.shape, 0) * 128 + lax.broadcasted_iota(
        jnp.int32, code_v.shape, 1
    )
    for load in loads[:4]:
        load.wait()

    def note(t, packed):
        code = left[0, 0, t] * xt + right[0, 0, t] + 1
        return jnp.where(tile_id == dest[0, 0, t], packed * (1 << width) + code, packed)

    code_v[...] = lax.fori_loop(0, count, note, jnp.zeros(code_v.shape, jnp.int32), unroll=8)
    codes = pltpu.make_async_copy(code_v, code_s, code_sem)
    codes.start()
    flag[...] = jnp.full(flag.shape, slot[0, 0], jnp.int32)

    prod[0] = jnp.zeros((edge, edge), f32)
    prod[1 + pairs] = jnp.zeros((edge, edge), f32)
    turn = permutation(edge, 1)
    loads[4].wait()
    loads[5].wait()
    a = split2(t2[...].reshape(xt * edge, t2.shape[2]))
    a_turned = [
        jnp.concatenate([turned(turn, x[l * edge : (l + 1) * edge]) for l in range(xt)], axis=0) for x in a
    ]
    for r in range(0, xt, 2):
        sides = [split2(ints[r + d]) for d in range(2)]
        b = [jnp.concatenate([sides[0][k], sides[1][k]], axis=1) for k in range(2)]
        b_turned = [
            jnp.concatenate([turned(sides[0][k], turn), turned(sides[1][k], turn)], axis=1) for k in range(2)
        ]
        for base, res in ((1, dot3(a, b)), (2 + pairs, dot3(a_turned, b_turned))):
            for l in range(xt):
                for d in range(2):
                    prod[base + l * xt + r + d] = res[l * edge : (l + 1) * edge, d * edge : (d + 1) * edge]
    codes.wait()

    def place(c, rel):
        return sum(1 << h for h in range(levels) if rel & orders[c][h])

    def assemble(rel):
        home = cls
        for bit in turns:
            if rel & bit:
                home = home + turns[bit]
        ids = []
        for j in range(2 * owned):
            g = (home if j < owned else n_occ - 1 - home) * owned + j % owned
            packed = code_s[0, g] if code_s.shape[0] == 1 else code_s[lax.div(g, 128), lax.rem(g, 128)]
            base = 0 if j < owned else 1 + pairs
            ids.append([base + (lax.shift_right_logical(packed, width * k) & ((1 << width) - 1)) for k in range(CAP)])
        for c in range(CHUNKS):
            lo, half = chunks[c]
            i = place(c, rel)
            for at, row in ((0, lo), (half, edge - lo - half)):
                low0, low1, up0, up1 = [
                    prod[k[0], row : row + half, :] + prod[k[1], row : row + half, :] + prod[k[2], row : row + half, :]
                    for k in ids
                ]
                acc[c][i, 0, at : at + half, :] = low0 + up0
                acc[c][i, 1, at : at + half, :] = low0 + up1
                acc[c][i, 2, at : at + half, :] = low1 + up0
            if i >= blocks // 2:
                step_copy(c, i, levels - 1).start()

    def step_copy(c, i, h):
        return pltpu.make_async_remote_copy(
            src_ref=acc[c].at[i],
            dst_ref=got[c].at[i],
            send_sem=send_sem.at[c, i],
            recv_sem=recv_sem.at[c, i],
            device_id=(peers[orders[c][h]], q),
            device_id_type=MESH,
        )

    pl.semaphore_wait(barrier, bits + n_vir - 1)

    for rel in sorted(range(blocks), key=lambda r: -sum(r >> b & 1 for b in range(levels))):
        assemble(rel)

    flag_copy = pltpu.make_async_remote_copy(
        src_ref=flag, dst_ref=flag_got, send_sem=flag_send, recv_sem=flag_recv,
        device_id=(partner, q), device_id_type=MESH,
    )
    flag_copy.start()

    for load in loads[6:]:
        load.wait()
    for s in range(owned):
        for b in range(mask.shape[1]):
            rows, cols = pl.ds(s * edge, edge), pl.ds(b * edge, edge)
            hi, lo = split2(lam[rows, cols] * mask[s, b].astype(f32))
            lam_hi[rows, cols] = hi
            lam_lo[rows, cols] = lo

    def ladder(column):
        cols = pl.ds(pl.multiple_of(column * edge, edge), edge)
        return dot3((lam_hi[...], lam_lo[...]), split2(lints[:, cols]))

    lad_copies = []
    for off in range(1, n_vir):
        column = lax.rem(q + off, n_vir)
        lad[off] = ladder(column)
        lad_copies.append(
            pltpu.make_async_remote_copy(
                src_ref=lad.at[off], dst_ref=lad_got.at[off - 1],
                send_sem=lad_send.at[off - 1], recv_sem=lad_recv.at[off - 1],
                device_id=(p, column), device_id_type=MESH,
            )
        )
        lad_copies[-1].start()
    lad[0] = ladder(q)
    lanes = permutation(edge, upper)

    def add_ladder():
        for copy in lad_copies:
            copy.wait_recv()
        total = lad[0]
        for off in range(1, n_vir):
            total = total + lad_got[off - 1]
        for s in range(owned):
            y = None
            for piece in split3(total[s * edge : (s + 1) * edge]):
                part = dot(lanes, turned(piece, lanes))
                y = part if y is None else y + part
            lad[0, s * edge : (s + 1) * edge, :] = y
        for c in range(CHUNKS):
            lo, half = chunks[c]
            for at, row in ((0, lo), (half, edge - lo - half)):
                here = pl.ds(at, half)
                for j, s in ((0, 0), (1, upper), (2, 1 - upper)):
                    acc[c][0, j, here, :] = acc[c][0, j, here, :] + lad[0, pl.ds(pl.multiple_of(s * edge + row, 8), half), :]

    def take(c, i, h):
        for k in range(h, levels):
            step_copy(c, i + (1 << k), k).wait_recv()
            acc[c][i] = acc[c][i] + got[c][i + (1 << k)]

    def fin_copy(c):
        return pltpu.make_async_remote_copy(
            src_ref=fin[c], dst_ref=fin_got[c], send_sem=fin_send.at[c], recv_sem=fin_recv.at[c],
            device_id=(partner, q), device_id_type=MESH,
        )

    def finish(c):
        m = 2 * chunks[c][1]
        take(c, 0, 0)
        for target, which, swap in ((fin[c], 1 - upper, flag_got), (own[c], upper, flag)):
            keep = jnp.broadcast_to(swap[0:1, :] == 0, (m, edge))
            first, second = acc[c][0, 1 + which], acc[c][0, 2 - which]
            target[0] = jnp.where(keep, acc[c][0, 0], first)
            target[1] = jnp.where(keep, (first - acc[c][0, 0]) + second, second)
            if target is fin[c]:
                fin_copy(c).start()

    for h in reversed(range(levels - 1)):
        if h == 0:
            add_ladder()
        for i in reversed(range(1 << h, 2 << h)):
            for c in range(CHUNKS):
                take(c, i, h + 1)
                step_copy(c, i, h).start()

    flag_copy.wait_recv()
    for c in range(CHUNKS):
        finish(c)

    for c in range(CHUNKS):
        lo, half = chunks[c]
        size = 2 * owned * half
        rows = permutation(size, 1)
        fin_copy(c).wait_recv()

        @pl.when(upper == 0)
        def _():
            for s in range(owned):
                for at, row in ((0, lo), (half, edge - lo - half)):
                    out[s * edge + row : s * edge + row + half, :] = (
                        own[c][s, at : at + half, :] + fin_got[c][s, at : at + half, :]
                    )

        @pl.when(upper == 1)
        def _():
            y = None
            for piece in split3((own[c][...] + fin_got[c][...]).reshape(size, edge)):
                part = dot(rows, turned(piece, turn))
                y = part if y is None else y + part
            y = y.reshape(owned, 2 * half, edge)
            for s in range(owned):
                for at, row in ((0, lo), (half, edge - lo - half)):
                    out[s * edge + row : s * edge + row + half, :] = y[owned - 1 - s, at : at + half, :]

    flag_copy.wait_send()
    for copy in lad_copies:
        copy.wait_send()
    for c in range(CHUNKS):
        fin_copy(c).wait_send()
        for h in range(levels):

            @pl.loop(1 << h, 2 << h)
            def _(i):
                step_copy(c, i, h).wait_send()


def body(
    n_occ, n_vir,
    t2_tiles, cycle_ints, cycle_left, cycle_right, cycle_dest, lam_ladder, ladder_ints, ladder_mask, partner_slot, denom,
):
    edge = denom.shape[1]
    owned = partner_slot.shape[1]
    xt, kc = cycle_ints.shape[2], cycle_ints.shape[3]
    blocks = n_occ // 2
    chunks = chunk_plan(edge)
    tiles = n_occ * owned
    code_rows = -(-tiles // 128)
    rows = owned * edge
    per_chunk = lambda *lead: tuple(pltpu.VMEM((*lead, 2 * half, edge), f32) for _, half in chunks)
    sem = pltpu.SemaphoreType.DMA
    hbm = pl.BlockSpec(memory_space=pltpu.HBM)
    smem = lambda x: pltpu.SMEM(x.shape, x.dtype)
    sym = pl.pallas_call(
        functools.partial(kernel, n_occ, n_vir, chunks),
        out_shape=pltpu.VMEM((rows, edge), f32),
        in_specs=[hbm] * 9,
        out_specs=pl.BlockSpec(memory_space=pltpu.VMEM),
        scratch_shapes=[
            smem(cycle_left),
            smem(cycle_right),
            smem(cycle_dest),
            smem(ladder_mask),
            smem(partner_slot),
            pltpu.VMEM((xt, edge, kc), f32),
            pltpu.VMEM((xt, kc, edge), f32),
            pltpu.VMEM(lam_ladder.shape, f32),
            pltpu.VMEM(ladder_ints.shape, f32),
            pltpu.VMEM((code_rows, 128), jnp.int32),
            pltpu.SMEM((code_rows, 128), jnp.int32),
            pltpu.VMEM((2 + 2 * xt * xt, edge, edge), f32),
            pltpu.VMEM(lam_ladder.shape, bf16),
            pltpu.VMEM(lam_ladder.shape, bf16),
            pltpu.VMEM((n_vir, rows, edge), f32),
            pltpu.VMEM((n_vir - 1, rows, edge), f32),
            pltpu.VMEM((8, 128), jnp.int32),
            pltpu.VMEM((8, 128), jnp.int32),
            (
                per_chunk(blocks, 3), per_chunk(blocks, 3),
                per_chunk(owned), per_chunk(owned), per_chunk(owned),
            ),
            sem((9,)),
            sem,
            sem((CHUNKS, blocks)),
            sem((CHUNKS, blocks)),
            sem((CHUNKS,)),
            sem((CHUNKS,)),
            sem((n_vir - 1,)),
            sem((n_vir - 1,)),
            sem,
            sem,
        ],
        compiler_params=pltpu.CompilerParams(
            collective_id=0, has_side_effects=True, vmem_limit_bytes=56 * 1024 * 1024
        ),
        cost_estimate=pl.CostEstimate(flops=10**9, bytes_accessed=4 * 10**6, transcendentals=0),
    )(cycle_left, cycle_right, cycle_dest, ladder_mask, partner_slot, t2_tiles, cycle_ints, lam_ladder, ladder_ints)
    return sym / denom


def solution(mesh):
    in_specs = (
        P("occ", "vir", None, None, None),
        P("occ", "vir", None, None, None),
        P("occ", "vir", None),
        P("occ", "vir", None),
        P("occ", "vir", None),
        P("occ", "vir"),
        P("vir", None),
        P("occ", "vir"),
        P("occ", None),
        P("occ", "vir"),
    )
    local = functools.partial(body, mesh.shape["occ"], mesh.shape["vir"])
    return jax.shard_map(local, mesh=mesh, in_specs=in_specs, out_specs=P("occ", "vir"), check_vma=False)
```
